256 devices in a mesh: runs: 8 (over z_lo, y), cells: 32 (over x, z_hi, core).
Axes of the slice: x: 4, y: 4, z: 8 (z_hi: 4, z_lo: 2; z = z_hi * 2 + z_lo), core: 2. Of those that a mesh axis runs over, the one named last changes fastest.
Arguments:
- fields: bfloat16 [64, 120, 65536], P('runs', None, 'cells'), may hold values from -100 to 100, as said below
- vectors: bfloat16 [64, 120, 48], P('runs'), may hold values from -1 to 1, as said below
- combos: bfloat16 [3072, 64], replicated, may hold values from -0.109375 to 0.109375
Outputs:
- gram: float32 [64, 120, 120], P('runs')
- basis: bfloat16 [3072, 65536], P('runs', 'cells')
- merged: float32 [3072, 3072], P('runs')
- eofs: bfloat16 [64, 65536], P(None, 'cells')
- pcs: float32 [64, 120, 64], P('runs')
The draws below stay inside these ranges and needn't reach their ends.
Inputs may be any that keep to these rules, and one draw needn't show every extreme that they name: `fields`: each run shares a field with all others beside its own; the grid cells carry different scales. `vectors`: columns are not orthonormal.
All inputs are finite; a program needn't handle non-finite values.
Results may differ from the reference program's by a relative error of at most 0.0058.
Values may be sent and summed in bfloat16 or wider, within the bound.
No kernel may reach another device: no remote copies, remote signals or barrier semaphores. Data moves between devices by JAX's collectives and lax.ppermute only.
A program may use at most 64 MiB of HBM per device.

```python
import math
import jax
import jax.numpy as jnp
from jax import lax

MONTHS = 120
MODES = 48
COMMON = 64
CELL_DEV = 2048
RUNS = 64
CELLS = 65536


def draw_fields(key, part):
    key = jax.random.fold_in(key, 11)
    keys = jax.random.split(key, 5)
    position = jnp.arange(CELLS, dtype=jnp.float32) / CELLS
    shared = jax.random.normal(keys[0], (MONTHS, CELLS), jnp.float32)
    own = jax.random.normal(keys[1], (RUNS, MONTHS, CELLS), jnp.float32)
    cell_scale = jnp.exp(math.log(3.0) * position + jax.random.uniform(keys[2], (CELLS,), jnp.float32, 0.0, math.log(2.0)))
    block_of = jnp.arange(CELLS, dtype=jnp.int32) // CELL_DEV
    chosen = jax.random.randint(keys[4], (CELLS // CELL_DEV,), 0, RUNS, dtype=jnp.int32)
    owner = jnp.take(chosen, block_of)
    boost = jnp.where(jnp.arange(RUNS, dtype=jnp.int32)[:, None] == owner[None, :], 4.0, 1.0).astype(jnp.float32)
    values = boost[:, None, :] * cell_scale * (0.8 * shared[None] + 0.6 * own)
    return jnp.clip(values, -100.0, 100.0).astype(jnp.bfloat16)


def draw_vectors(key, part):
    key = jax.random.fold_in(key, 12)
    keys = jax.random.split(key, 2)
    shared = jax.random.normal(keys[0], (MONTHS, MODES), jnp.float32)
    own = jax.random.normal(keys[1], (RUNS, MONTHS, MODES), jnp.float32)
    values = (0.8 * shared[None] + 0.6 * own) / math.sqrt(MONTHS)
    return jnp.clip(values, -1.0, 1.0).astype(jnp.bfloat16)


def centred(rng, dims, deviation, most, kind=jnp.bfloat16):
    result = deviation * jax.random.normal(rng, dims, jnp.float32)
    return jnp.clip(result, min=-most, max=most).astype(kind)


def setup_inputs(seed: int = 0) -> dict:
    splits = jax.random.split(jax.random.key(seed), 4)
    return {
        "fields": draw_fields(jax.random.fold_in(splits[3], 71), 0),
        "vectors": draw_vectors(jax.random.fold_in(splits[3], 71), 0),
        "combos": centred(splits[2], (RUNS * MODES, COMMON), (RUNS * MODES) ** -0.5, 0.109375),
    }


def reference(fields, vectors, combos):
    runs, months, cells = fields.shape
    modes = vectors.shape[2]
    wide = fields.astype(jnp.float32)
    gram = jnp.einsum('rmc,rnc->rmn', wide, wide, precision=lax.Precision.HIGHEST) / cells
    vec_wide = vectors.astype(jnp.float32)
    scale = jnp.einsum('rmk,rmn,rnk->rk', vec_wide, gram, vec_wide, precision=lax.Precision.HIGHEST)
    projected = jnp.einsum('rmk,rmc->rkc', vec_wide, wide, precision=lax.Precision.HIGHEST)
    basis = (projected / jnp.sqrt(scale)[:, :, None]).astype(jnp.bfloat16).reshape(runs * modes, cells)
    merged = jnp.dot(basis, basis.T, preferred_element_type=jnp.float32) / cells
    mode = jnp.dot(combos.T, basis, preferred_element_type=jnp.float32).astype(jnp.bfloat16)
    comb_wide = combos.astype(jnp.float32)
    norms = lax.optimization_barrier(jnp.sum(comb_wide * jnp.dot(merged, comb_wide, precision=lax.Precision.HIGHEST), axis=0))
    root = jnp.sqrt(norms)
    mode_wide = mode.astype(jnp.float32)
    eofs = (mode_wide / root[:, None]).astype(jnp.bfloat16)
    pcs = jnp.einsum('rmc,jc->rmj', wide, mode_wide, precision=lax.Precision.HIGHEST) / (cells * root)
    return (gram, basis, merged, eofs, pcs)
```

```python
import jax
import jax.numpy as jnp
from jax import lax
from jax.experimental import pallas as pl
from jax.experimental.pallas import tpu as pltpu
from jax.sharding import Mesh
from jax.sharding import PartitionSpec as P

RUNS = ("z_lo", "y")
CELLS = ("x", "z_hi", "core")
F32 = jnp.float32
BF16 = jnp.bfloat16
PARAMS = pltpu.CompilerParams(vmem_limit_bytes=40 << 20)


def send_to(x, da, db):
    pairs = [
        (a * 4 + b, (a + da) % 2 * 4 + (b + db) % 4) for a in range(2) for b in range(4)
    ]
    return lax.ppermute(x, RUNS, pairs)


def swap_cores(x):
    return lax.ppermute(x, "core", [(0, 1), (1, 0)])


def spread(x, axes):
    n = lax.axis_size(axes)
    return lax.all_to_all(jnp.broadcast_to(x[None], (n,) + x.shape), axes, 0, 0, tiled=True)


def rows_times(a, b):
    return lax.dot_general(a, b, (((1,), (1,)), ((), ())), preferred_element_type=F32)


def times_rows(a, b):
    return lax.dot_general(a, b, (((0,), (0,)), ((), ())), preferred_element_type=F32)


def project_kernel(spot, fields, vectors, left, right, far, squares):
    value = times_rows(vectors[0], fields[0])
    squares[0] = jnp.sum(value * value, axis=1, keepdims=True)
    value = value.astype(BF16)
    half = value.shape[1] // 2
    left[...] = value[:, :half]
    right[...] = value[:, half:]
    far[...] = jnp.where(spot[1] // 2 == 0, value[:, half:], value[:, :half])


def project(spot, fields, vectors):
    runs, months, cells = fields.shape
    modes = vectors.shape[2]
    half = pl.BlockSpec((modes, cells // 2), lambda r, spot: (r, 0))
    out = jax.ShapeDtypeStruct((runs * modes, cells // 2), BF16)
    return pl.pallas_call(
        project_kernel,
        grid_spec=pltpu.PrefetchScalarGridSpec(
            num_scalar_prefetch=1,
            grid=(runs,),
            in_specs=[
                pl.BlockSpec((1, months, cells), lambda r, spot: (r, 0, 0)),
                pl.BlockSpec((1, months, modes), lambda r, spot: (r, 0, 0)),
            ],
            out_specs=[half] * 3 + [pl.BlockSpec((1, modes, 1), lambda r, spot: (r, 0, 0))],
        ),
        out_shape=[out] * 3 + [jax.ShapeDtypeStruct((runs, modes, 1), F32)],
        cost_estimate=pl.CostEstimate(
            flops=2 * runs * months * modes * cells,
            bytes_accessed=fields.size * 4,
            transcendentals=0,
        ),
        compiler_params=PARAMS,
    )(spot, fields, vectors)


def gram_kernel(fields, gram):
    months = fields.shape[1]
    gram[0] = jnp.zeros_like(gram[0])
    gram[0, :months, :months] = rows_times(fields[0], fields[0])


def gram_of(fields):
    runs, months, cells = fields.shape
    return pl.pallas_call(
        gram_kernel,
        grid=(runs,),
        in_specs=[pl.BlockSpec((1, months, cells), lambda r: (r, 0, 0))],
        out_specs=pl.BlockSpec((1, 128, 128), lambda r: (r, 0, 0)),
        out_shape=jax.ShapeDtypeStruct((runs, 128, 128), F32),
        cost_estimate=pl.CostEstimate(
            flops=2 * runs * months * months * cells,
            bytes_accessed=fields.size * 2,
            transcendentals=0,
        ),
        compiler_params=PARAMS,
    )(fields)


def pcs_kernel(first, second, mode, norms, out):
    months, common = first.shape[1], mode.shape[0]
    out[0] = jnp.zeros_like(out[0])
    out[0, :months, :common] = rows_times(first[0], mode[...])
    out[0, :months, common:] = rows_times(second[0], mode[...])
    out[0, months : months + 1, :] = norms[...]


def pcs_of(fields, mode, norms):
    runs, months, cells = fields.shape
    return pl.pallas_call(
        pcs_kernel,
        grid=(runs // 2,),
        in_specs=[
            pl.BlockSpec((1, months, cells), lambda r: (r, 0, 0)),
            pl.BlockSpec((1, months, cells), lambda r: (r + 4, 0, 0)),
            pl.BlockSpec(mode.shape, lambda r: (0, 0)),
            pl.BlockSpec(norms.shape, lambda r: (0, 0)),
        ],
        out_specs=pl.BlockSpec((1, 128, 128), lambda r: (r, 0, 0)),
        out_shape=jax.ShapeDtypeStruct((runs // 2, 128, 128), F32),
        cost_estimate=pl.CostEstimate(
            flops=2 * fields.size * mode.shape[0],
            bytes_accessed=fields.size * 2,
            transcendentals=0,
        ),
        compiler_params=PARAMS,
    )(fields, fields, mode, norms)


def put(spot, run, value, keep, send):
    value = value.astype(BF16)
    rows = value.shape[0]
    size = rows // 8

    def store(first, second):
        for x in range(4):
            for k in range(rows // 128):
                at = run * (rows // 128) + k
                columns = slice(k * 128, (k + 1) * 128)
                first[x, at] = value[x * size : (x + 1) * size, columns]
                second[x, at] = value[(x + 4) * size : (x + 5) * size, columns]

    @pl.when(spot[2] == 0)
    def _():
        store(keep, send)

    @pl.when(spot[2] != 0)
    def _():
        store(send, keep)


def put_product(spot, run, swapped, mine, theirs, keep, send):
    @pl.when(swapped == 0)
    def _():
        put(spot, run, rows_times(mine, theirs), keep, send)

    @pl.when(swapped != 0)
    def _():
        put(spot, run, rows_times(theirs, mine), keep, send)


def wrap(x):
    return lax.rem(x + 4, 4)


def chosen(flag, left, right):
    return jnp.where(flag == 0, left[...], right[...])


def blocks_kernel(
    spot, left, right, down, up, over, z_left, z_right, z_down, z_up, z_over, keep, send
):
    a, b = spot[0], spot[1]
    own = rows_times(left[...], left[...]) + rows_times(right[...], right[...])
    put(spot, a * 4 + b, own, keep, send)
    below, above, across = wrap(b + 1), wrap(b - 1), wrap(b + 2)
    middle = chosen(b // 2, left, right)
    beside = chosen(a, z_left, z_right)
    for run, swapped, mine, theirs in (
        (a * 4 + below, (below < b).astype(jnp.int32), left[...], down),
        (a * 4 + above, (above < b).astype(jnp.int32), right[...], up),
        (a * 4 + across, b // 2, middle, over),
        (4 - a * 4 + b, a, chosen(a, left, right), beside),
        (4 - a * 4 + below, a, left[...], z_down),
        (4 - a * 4 + above, a, right[...], z_up),
        (4 - a * 4 + across, a, middle, z_over),
    ):
        put_product(spot, run, swapped, mine, theirs[...], keep, send)


def blocks_of(spot, left, *others):
    rows, cells = left.shape
    out = jax.ShapeDtypeStruct((4, 8 * rows // 128, rows // 8, 128), BF16)
    whole = pl.BlockSpec(memory_space=pltpu.VMEM)
    return pl.pallas_call(
        blocks_kernel,
        in_specs=[pl.BlockSpec(memory_space=pltpu.SMEM)] + [whole] * (1 + len(others)),
        out_specs=[whole, whole],
        out_shape=[out, out],
        cost_estimate=pl.CostEstimate(
            flops=18 * rows * rows * cells, bytes_accessed=24 * left.size, transcendentals=0
        ),
        compiler_params=PARAMS,
    )(spot, left, *others)


def assemble_kernel(spot, own, other, row, col, out):
    j = pl.program_id(0)
    mine = spot[0] * 4 + spot[1]
    rows = out.shape[0]
    size, slabs = rows // 8, rows // 128
    here = pl.ds(pl.multiple_of(lax.rem(j, 2) * size * slabs, 16), size * slabs)
    parts = []
    for core in range(2):
        for x in range(4):
            held = jnp.where(spot[2] == core, own[x, 0, here], other[x, 0, here])
            parts.append(
                jnp.concatenate([held[k * size : (k + 1) * size] for k in range(slabs)], axis=1)
            )
    value = jnp.concatenate(parts, axis=0).astype(F32)

    @pl.when(j >= mine)
    def _():
        out[...] = value * row[...] * col[0]

    @pl.when(j < mine)
    def _():
        out[...] = value.T * row[...] * col[0]


def assemble(spot, own, other, row, col):
    rows = row.shape[0]
    held = pl.BlockSpec((4, 1) + own.shape[2:], lambda j, spot: (0, j // 2, 0, 0))
    return pl.pallas_call(
        assemble_kernel,
        grid_spec=pltpu.PrefetchScalarGridSpec(
            num_scalar_prefetch=1,
            grid=(8,),
            in_specs=[
                held,
                held,
                pl.BlockSpec((rows, 1), lambda j, spot: (0, 0)),
                pl.BlockSpec((1, 1, rows), lambda j, spot: (j, 0, 0)),
            ],
            out_specs=pl.BlockSpec((rows, rows), lambda j, spot: (0, j)),
        ),
        out_shape=jax.ShapeDtypeStruct((rows, 8 * rows), F32),
        compiler_params=PARAMS,
    )(spot, own, other, row, col)


def sum_of(parts):
    return jnp.sum(parts.astype(F32), axis=0)


def split(x):
    high = lax.reduce_precision(x, 8, 7)
    return jnp.concatenate([high.astype(BF16), (x - high).astype(BF16)], axis=0)


def scatter_x(parts):
    return sum_of(lax.all_to_all(parts, "x", 0, 0, tiled=True))


def together(work, *arrays):
    def nothing(*arrays):
        return jax.tree.map(lambda x: jnp.zeros(x.shape, x.dtype), jax.eval_shape(work, *arrays))

    return lax.cond(lax.axis_index("core") < 2, work, nothing, *arrays)


def per_device(fields, vectors, combos):
    runs, months, cells = fields.shape
    modes = vectors.shape[2]
    common = combos.shape[1]
    rows = runs * modes
    total = cells * lax.axis_size(CELLS)
    a, b, core = (lax.axis_index(name) for name in ("z_lo", "y", "core"))
    spot = jnp.stack([a, b, core]).astype(jnp.int32)
    barrier = lax.optimization_barrier

    left, right, far, squares = project(spot, fields, vectors)
    near = (send_to(left, 0, -1), send_to(right, 0, 1), send_to(far, 0, 2))
    z_left, z_right = send_to(left, 1, 0), send_to(right, 1, 0)
    weights = lax.dynamic_slice_in_dim(combos, lax.axis_index(RUNS) * rows, rows, 0)

    def scale_work(squares):
        scale = jnp.sum(spread(squares.reshape(3, rows // 3), CELLS), axis=0)
        return scale.reshape(runs, modes) / total

    def mode_work(fields, vectors, weights, scale):
        projected = jnp.einsum("rmk,rmc->rkc", vectors, fields, preferred_element_type=F32)
        basis = (projected * lax.rsqrt(scale)[:, :, None]).astype(BF16).reshape(rows, cells)
        part = times_rows(weights, basis).reshape(8, common // 8, cells)
        part = jnp.concatenate([part, jnp.broadcast_to(scale[None], (8, runs, modes))], axis=2)
        part = lax.all_to_all(part, RUNS, 0, 0, tiled=True)
        return basis, part, gram_of(fields)

    scale = together(scale_work, squares)
    scale, z_left, z_right, *near = barrier((scale, z_left, z_right, *near))
    z_over = jnp.where(b // 2 == 0, z_right, z_left)
    far = (send_to(z_left, 0, -1), send_to(z_right, 0, 1), send_to(z_over, 0, 2))
    basis, part, gram = together(mode_work, fields, vectors, weights, scale)
    part, *far = barrier((part, *far))

    scales = part[:, :, cells:].reshape(8, rows)
    mode = spread(jnp.sum(part[:, :, :cells], axis=0).astype(BF16), RUNS)
    keep, send = blocks_of(spot, left, right, *near, z_left, z_right, *far)
    blocks = (keep.astype(F32) + swap_cores(send).astype(F32)).astype(BF16)
    gram_keep = jnp.where(core == 0, gram[:4], gram[4:])
    gram_send = jnp.where(core == 0, gram[4:], gram[:4])
    gram = (gram_keep + swap_cores(gram_send)).astype(BF16)
    mode = mode.reshape(common, cells)
    mode_wide = mode.astype(F32)
    norms = jnp.sum(mode_wide * mode_wide, axis=1) / total
    norms = jnp.concatenate([norms, norms])[None]
    pcs = pcs_of(fields, mode, norms)
    pcs_keep = jnp.where(core == 0, pcs[:2], pcs[2:])
    pcs_send = jnp.where(core == 0, pcs[2:], pcs[:2])
    pcs = split(pcs_keep + swap_cores(pcs_send))
    extra = jnp.concatenate([gram, pcs], axis=0)
    extra = extra.reshape(8, 4, 32, 128).transpose(1, 0, 2, 3).reshape(4, 256, 128)

    half = rows * 3
    blocks = scatter_x(jnp.concatenate([blocks.reshape(4, half, 128), extra], axis=1))
    extra, blocks = blocks[half:], blocks[:half].astype(BF16).reshape(8, half // 8, 128)
    others = lax.all_to_all(blocks, RUNS, 0, 0, tiled=True)
    same = lax.broadcasted_iota(jnp.int32, (8, 1, 1), 0) == a * 4 + b
    others = jnp.where(same, 0.0, others.astype(F32))
    blocks = (blocks.astype(F32) + others).astype(BF16).reshape(4, half // 4, 128)
    pcs = split(extra[128:192] + extra[192:]).reshape(2, 4, 16, 128)
    pieces = [blocks, extra[:128].astype(BF16).reshape(4, 32, 128), pcs[0], pcs[1]]
    pieces = jnp.concatenate(pieces, axis=1)
    pieces = sum_of(lax.all_to_all(pieces, "z_hi", 0, 0, tiled=True))
    pcs = split(pieces[-32:-16] + pieces[-16:])
    pieces = jnp.concatenate([pieces[:-32].astype(BF16), pcs], axis=0)
    own = spread(spread(pieces, "z_hi"), "x")
    other = swap_cores(own)
    row = lax.rsqrt(scale).reshape(rows, 1) / total
    col = lax.rsqrt(scales).reshape(8, 1, rows)
    merged = assemble(spot, own, other, row, col)

    def whole(pieces):
        extra = pieces[:, :, -64:].astype(F32)
        gram = extra[:, :, :32].transpose(1, 0, 2, 3).reshape(4, 128, 128)
        pcs = extra[:, :, 32:48] + extra[:, :, 48:]
        pcs = pcs.reshape(4, 2, 2, 16, 128).transpose(1, 0, 2, 3, 4).reshape(2, 128, 128)
        return gram, pcs

    both = [whole(own), whole(other)]
    gram, pcs = (
        jnp.where(
            core == 0,
            jnp.concatenate([both[0][n], both[1][n]]),
            jnp.concatenate([both[1][n], both[0][n]]),
        )
        for n in range(2)
    )
    gram = gram[:, :months, :months] / total
    inverse = lax.rsqrt(pcs[0, months])
    pcs = pcs[:, :months] * inverse / total
    pcs = jnp.concatenate([pcs[:, :, :common], pcs[:, :, common:]], axis=0)
    eofs = (mode_wide * inverse[:common, None]).astype(BF16)
    return (gram, basis, merged, eofs, pcs)


def solution(mesh):
    fine = Mesh(mesh.devices.reshape(2, 4, 4, 4, 2), RUNS + CELLS)
    return jax.shard_map(
        per_device,
        mesh=fine,
        in_specs=(P(RUNS, None, CELLS), P(RUNS, None, None), P()),
        out_specs=(
            P(RUNS, None, None),
            P(RUNS, CELLS),
            P(RUNS, None),
            P(None, CELLS),
            P(RUNS, None, None),
        ),
        check_vma=False,
    )
```

```python
import jax
import jax.numpy as jnp
from jax import lax
from jax.experimental import pallas as pl
from jax.experimental.pallas import tpu as pltpu
from jax.sharding import Mesh
from jax.sharding import PartitionSpec as P

RUNS = ("z_lo", "y")
CELLS = ("x", "z_hi", "core")
F32 = jnp.float32
BF16 = jnp.bfloat16
PARAMS = pltpu.CompilerParams(vmem_limit_bytes=40 << 20)


def send_to(x, da, db):
    pairs = [
        (a * 4 + b, (a + da) % 2 * 4 + (b + db) % 4) for a in range(2) for b in range(4)
    ]
    return lax.ppermute(x, RUNS, pairs)


def swap_cores(x):
    return lax.ppermute(x, "core", [(0, 1), (1, 0)])


def spread(x, axes):
    n = lax.axis_size(axes)
    return lax.all_to_all(jnp.broadcast_to(x[None], (n,) + x.shape), axes, 0, 0, tiled=True)


def rows_times(a, b):
    return lax.dot_general(a, b, (((1,), (1,)), ((), ())), preferred_element_type=F32)


def times_rows(a, b):
    return lax.dot_general(a, b, (((0,), (0,)), ((), ())), preferred_element_type=F32)


def project_kernel(spot, fields, vectors, left, right, far, squares):
    value = times_rows(vectors[0], fields[0])
    squares[0] = jnp.sum(value * value, axis=1, keepdims=True)
    value = value.astype(BF16)
    half = value.shape[1] // 2
    left[...] = value[:, :half]
    right[...] = value[:, half:]
    far[...] = jnp.where(spot[1] // 2 == 0, value[:, half:], value[:, :half])


def project(spot, fields, vectors):
    runs, months, cells = fields.shape
    modes = vectors.shape[2]
    half = pl.BlockSpec((modes, cells // 2), lambda r, spot: (r, 0))
    out = jax.ShapeDtypeStruct((runs * modes, cells // 2), BF16)
    return pl.pallas_call(
        project_kernel,
        grid_spec=pltpu.PrefetchScalarGridSpec(
            num_scalar_prefetch=1,
            grid=(runs,),
            in_specs=[
                pl.BlockSpec((1, months, cells), lambda r, spot: (r, 0, 0)),
                pl.BlockSpec((1, months, modes), lambda r, spot: (r, 0, 0)),
            ],
            out_specs=[half] * 3 + [pl.BlockSpec((1, modes, 1), lambda r, spot: (r, 0, 0))],
        ),
        out_shape=[out] * 3 + [jax.ShapeDtypeStruct((runs, modes, 1), F32)],
        cost_estimate=pl.CostEstimate(
            flops=2 * runs * months * modes * cells,
            bytes_accessed=fields.size * 4,
            transcendentals=0,
        ),
        compiler_params=PARAMS,
    )(spot, fields, vectors)


def gram_kernel(fields, gram):
    months = fields.shape[1]
    gram[0] = jnp.zeros_like(gram[0])
    gram[0, :months, :months] = rows_times(fields[0], fields[0])


def gram_of(fields):
    runs, months, cells = fields.shape
    return pl.pallas_call(
        gram_kernel,
        grid=(runs,),
        in_specs=[pl.BlockSpec((1, months, cells), lambda r: (r, 0, 0))],
        out_specs=pl.BlockSpec((1, 128, 128), lambda r: (r, 0, 0)),
        out_shape=jax.ShapeDtypeStruct((runs, 128, 128), F32),
        cost_estimate=pl.CostEstimate(
            flops=2 * runs * months * months * cells,
            bytes_accessed=fields.size * 2,
            transcendentals=0,
        ),
        compiler_params=PARAMS,
    )(fields)


def pcs_kernel(first, second, mode, out):
    months, common = first.shape[1], mode.shape[0]
    wide = mode[...].astype(F32)
    norms = jnp.sum(wide * wide, axis=1, keepdims=True)
    out[0] = jnp.zeros_like(out[0])
    out[0, :common, :months] = rows_times(mode[...], first[0])
    out[0, common:, :months] = rows_times(mode[...], second[0])
    out[0, :common, months : months + 1] = norms
    out[0, common:, months : months + 1] = norms


def pcs_of(fields, mode):
    runs, months, cells = fields.shape
    return pl.pallas_call(
        pcs_kernel,
        grid=(runs // 2,),
        in_specs=[
            pl.BlockSpec((1, months, cells), lambda r: (r, 0, 0)),
            pl.BlockSpec((1, months, cells), lambda r: (r + 4, 0, 0)),
            pl.BlockSpec(mode.shape, lambda r: (0, 0)),
        ],
        out_specs=pl.BlockSpec((1, 128, 128), lambda r: (r, 0, 0)),
        out_shape=jax.ShapeDtypeStruct((runs // 2, 128, 128), F32),
        cost_estimate=pl.CostEstimate(
            flops=2 * fields.size * mode.shape[0],
            bytes_accessed=fields.size * 2,
            transcendentals=0,
        ),
        compiler_params=PARAMS,
    )(fields, fields, mode)


def put(spot, run, value, keep, send):
    value = value.astype(BF16)
    rows = value.shape[0]
    size = rows // 8

    def store(first, second):
        for x in range(4):
            for k in range(rows // 128):
                at = run * (rows // 128) + k
                columns = slice(k * 128, (k + 1) * 128)
                first[x, at] = value[x * size : (x + 1) * size, columns]
                second[x, at] = value[(x + 4) * size : (x + 5) * size, columns]

    @pl.when(spot[2] == 0)
    def _():
        store(keep, send)

    @pl.when(spot[2] != 0)
    def _():
        store(send, keep)


def put_product(spot, run, swapped, mine, theirs, keep, send):
    @pl.when(swapped == 0)
    def _():
        put(spot, run, rows_times(mine, theirs), keep, send)

    @pl.when(swapped != 0)
    def _():
        put(spot, run, rows_times(theirs, mine), keep, send)


def wrap(x):
    return lax.rem(x + 4, 4)


def chosen(flag, left, right):
    return jnp.where(flag == 0, left[...], right[...])


def near_kernel(spot, left, right, down, up, over, keep, send):
    b = spot[1]
    own = rows_times(left[...], left[...]) + rows_times(right[...], right[...])
    put(spot, b, own, keep, send)
    below, above, across = wrap(b + 1), wrap(b - 1), wrap(b + 2)
    middle = chosen(b // 2, left, right)
    for run, swapped, mine, theirs in (
        (below, (below < b).astype(jnp.int32), left[...], down),
        (above, (above < b).astype(jnp.int32), right[...], up),
        (across, b // 2, middle, over),
    ):
        put_product(spot, run, swapped, mine, theirs[...], keep, send)


def far_kernel(spot, left, right, z_left, z_right, down, up, over, keep, send):
    a, b = spot[0], spot[1]
    beside = chosen(a, z_left, z_right)
    middle = chosen(b // 2, left, right)
    for run, mine, theirs in (
        (b, chosen(a, left, right), beside),
        (wrap(b + 1), left[...], down[...]),
        (wrap(b - 1), right[...], up[...]),
        (wrap(b + 2), middle, over[...]),
    ):
        put_product(spot, run, a, mine, theirs, keep, send)


def blocks_of(kernel, spot, left, *others):
    rows, cells = left.shape
    out = jax.ShapeDtypeStruct((4, 4 * rows // 128, rows // 8, 128), BF16)
    whole = pl.BlockSpec(memory_space=pltpu.VMEM)
    return pl.pallas_call(
        kernel,
        in_specs=[pl.BlockSpec(memory_space=pltpu.SMEM)] + [whole] * (1 + len(others)),
        out_specs=[whole, whole],
        out_shape=[out, out],
        cost_estimate=pl.CostEstimate(
            flops=9 * rows * rows * cells, bytes_accessed=12 * left.size, transcendentals=0
        ),
        compiler_params=PARAMS,
    )(spot, left, *others)


def assemble_kernel(spot, own, other, row, col, out):
    j = pl.program_id(0)
    mine = spot[0] * 4 + spot[1]
    rows = out.shape[0]
    size, slabs = rows // 8, rows // 128
    here = pl.ds(pl.multiple_of(lax.rem(j, 2) * size * slabs, 16), size * slabs)
    parts = []
    for core in range(2):
        for x in range(4):
            held = jnp.where(spot[2] == core, own[x, 0, here], other[x, 0, here])
            parts.append(
                jnp.concatenate([held[k * size : (k + 1) * size] for k in range(slabs)], axis=1)
            )
    value = jnp.concatenate(parts, axis=0).astype(F32)

    @pl.when(j >= mine)
    def _():
        out[...] = value * row[...] * col[0]

    @pl.when(j < mine)
    def _():
        out[...] = value.T * row[...] * col[0]


def assemble(spot, own, other, row, col):
    rows = row.shape[0]
    held = pl.BlockSpec((4, 1) + own.shape[2:], lambda j, spot: (0, j // 2, 0, 0))
    return pl.pallas_call(
        assemble_kernel,
        grid_spec=pltpu.PrefetchScalarGridSpec(
            num_scalar_prefetch=1,
            grid=(8,),
            in_specs=[
                held,
                held,
                pl.BlockSpec((rows, 1), lambda j, spot: (0, 0)),
                pl.BlockSpec((1, 1, rows), lambda j, spot: (j, 0, 0)),
            ],
            out_specs=pl.BlockSpec((rows, rows), lambda j, spot: (0, j)),
        ),
        out_shape=jax.ShapeDtypeStruct((rows, 8 * rows), F32),
        compiler_params=PARAMS,
    )(spot, own, other, row, col)


def sum_of(parts):
    return jnp.sum(parts.astype(F32), axis=0)


def split(x):
    high = lax.reduce_precision(x, 8, 7)
    return jnp.concatenate([high.astype(BF16), (x - high).astype(BF16)], axis=0)


def scatter_x(parts):
    return sum_of(lax.all_to_all(parts, "x", 0, 0, tiled=True))


def together(work, *arrays):
    def nothing(*arrays):
        return jax.tree.map(lambda x: jnp.zeros(x.shape, x.dtype), jax.eval_shape(work, *arrays))

    return lax.cond(lax.axis_index("core") < 2, work, nothing, *arrays)


def per_device(fields, vectors, combos):
    runs, months, cells = fields.shape
    modes = vectors.shape[2]
    common = combos.shape[1]
    rows = runs * modes
    total = cells * lax.axis_size(CELLS)
    a, b, core = (lax.axis_index(name) for name in ("z_lo", "y", "core"))
    spot = jnp.stack([a, b, core]).astype(jnp.int32)
    barrier = lax.optimization_barrier

    left, right, far, squares = project(spot, fields, vectors)
    near = (send_to(left, 0, -1), send_to(right, 0, 1), send_to(far, 0, 2))
    z_left, z_right = send_to(left, 1, 0), send_to(right, 1, 0)
    weights = lax.dynamic_slice_in_dim(combos, lax.axis_index(RUNS) * rows, rows, 0)

    def scale_work(squares):
        scale = jnp.sum(spread(squares.reshape(3, rows // 3), CELLS), axis=0)
        return scale.reshape(runs, modes) / total

    def mode_work(fields, vectors, weights, scale, left, right, *near):
        keep, send = blocks_of(near_kernel, spot, left, right, *near)
        blocks = (keep.astype(F32) + swap_cores(send).astype(F32)).astype(BF16)
        blocks = scatter_x(blocks.reshape(4, rows * 3 // 2, 128)).astype(BF16)
        projected = jnp.einsum("rmk,rmc->rkc", vectors, fields, preferred_element_type=F32)
        basis = (projected * lax.rsqrt(scale)[:, :, None]).astype(BF16).reshape(rows, cells)
        part = times_rows(weights, basis).reshape(8, common // 8, cells)
        part = jnp.concatenate([part, jnp.broadcast_to(scale[None], (8, runs, modes))], axis=2)
        part, blocks = barrier((part, blocks))
        part = lax.all_to_all(part, RUNS, 0, 0, tiled=True)
        return basis, part, gram_of(fields), blocks

    scale = together(scale_work, squares)
    scale, z_left, z_right, *near = barrier((scale, z_left, z_right, *near))
    z_over = jnp.where(b // 2 == 0, z_right, z_left)
    far = (send_to(z_left, 0, -1), send_to(z_right, 0, 1), send_to(z_over, 0, 2))
    basis, part, gram, near = together(
        mode_work, fields, vectors, weights, scale, left, right, *near
    )
    part, near, *far = barrier((part, near, *far))

    scales = part[:, :, cells:].reshape(8, rows)
    mode = spread(jnp.sum(part[:, :, :cells], axis=0).astype(BF16), RUNS)
    keep, send = blocks_of(far_kernel, spot, left, right, z_left, z_right, *far)
    blocks = (keep.astype(F32) + swap_cores(send).astype(F32)).astype(BF16)
    gram_keep = jnp.where(core == 0, gram[:4], gram[4:])
    gram_send = jnp.where(core == 0, gram[4:], gram[:4])
    gram = (gram_keep + swap_cores(gram_send)).astype(BF16)
    mode = mode.reshape(common, cells)
    mode_wide = mode.astype(F32)
    pcs = pcs_of(fields, mode)
    pcs_keep = jnp.where(core == 0, pcs[:2], pcs[2:])
    pcs_send = jnp.where(core == 0, pcs[2:], pcs[:2])
    pcs = split(pcs_keep + swap_cores(pcs_send))
    extra = jnp.concatenate([gram, pcs], axis=0)
    extra = extra.reshape(8, 4, 32, 128).transpose(1, 0, 2, 3).reshape(4, 256, 128)

    half = rows * 3 // 2
    far = scatter_x(jnp.concatenate([blocks.reshape(4, half, 128), extra], axis=1))
    extra, far = far[half:], far[:half].astype(BF16)
    blocks = jnp.where(a == 0, jnp.concatenate([near, far]), jnp.concatenate([far, near]))
    blocks = blocks.reshape(8, half // 4, 128)
    others = lax.all_to_all(blocks, RUNS, 0, 0, tiled=True)
    same = lax.broadcasted_iota(jnp.int32, (8, 1, 1), 0) == a * 4 + b
    others = jnp.where(same, 0.0, others.astype(F32))
    blocks = (blocks.astype(F32) + others).astype(BF16).reshape(4, half // 2, 128)
    pcs = split(extra[128:192] + extra[192:]).reshape(2, 4, 16, 128)
    pieces = [blocks, extra[:128].astype(BF16).reshape(4, 32, 128), pcs[0], pcs[1]]
    pieces = jnp.concatenate(pieces, axis=1)
    pieces = sum_of(lax.all_to_all(pieces, "z_hi", 0, 0, tiled=True))
    pcs = split(pieces[-32:-16] + pieces[-16:])
    pieces = jnp.concatenate([pieces[:-32].astype(BF16), pcs], axis=0)
    own = spread(spread(pieces, "z_hi"), "x")
    other = swap_cores(own)
    row = lax.rsqrt(scale).reshape(rows, 1) / total
    col = lax.rsqrt(scales).reshape(8, 1, rows)
    merged = assemble(spot, own, other, row, col)

    def whole(pieces):
        extra = pieces[:, :, -64:].astype(F32)
        gram = extra[:, :, :32].transpose(1, 0, 2, 3).reshape(4, 128, 128)
        pcs = extra[:, :, 32:48] + extra[:, :, 48:]
        pcs = pcs.reshape(4, 2, 2, 16, 128).transpose(1, 0, 2, 3, 4).reshape(2, 128, 128)
        return gram, pcs

    both = [whole(own), whole(other)]
    gram, pcs = (
        jnp.where(
            core == 0,
            jnp.concatenate([both[0][n], both[1][n]]),
            jnp.concatenate([both[1][n], both[0][n]]),
        )
        for n in range(2)
    )
    gram = gram[:, :months, :months] / total
    pcs = pcs.reshape(runs // 2, 2, common, 128)
    inverse = lax.rsqrt(pcs[0, 0, :, months : months + 1] / total)
    pcs = (pcs[..., :months] * (inverse / total)).transpose(1, 0, 2, 3)
    pcs = pcs.reshape(runs, common, months).swapaxes(1, 2)
    eofs = (mode_wide * inverse).astype(BF16)
    return (gram, basis, merged, eofs, pcs)


def solution(mesh):
    fine = Mesh(mesh.devices.reshape(2, 4, 4, 4, 2), RUNS + CELLS)
    return jax.shard_map(
        per_device,
        mesh=fine,
        in_specs=(P(RUNS, None, CELLS), P(RUNS, None, None), P()),
        out_specs=(
            P(RUNS, None, None),
            P(RUNS, CELLS),
            P(RUNS, None),
            P(None, CELLS),
            P(RUNS, None, None),
        ),
        check_vma=False,
    )
```

```python
import jax
import jax.numpy as jnp
from jax import lax
from jax.experimental import pallas as pl
from jax.experimental.pallas import tpu as pltpu
from jax.sharding import Mesh
from jax.sharding import PartitionSpec as P

RUNS = ("z_lo", "y")
CELLS = ("x", "z_hi", "core")
F32 = jnp.float32
BF16 = jnp.bfloat16
PARAMS = pltpu.CompilerParams(vmem_limit_bytes=40 << 20)


def send_to(x, da, db):
    pairs = [
        (a * 4 + b, (a + da) % 2 * 4 + (b + db) % 4) for a in range(2) for b in range(4)
    ]
    return lax.ppermute(x, RUNS, pairs)


def swap_cores(x):
    return lax.ppermute(x, "core", [(0, 1), (1, 0)])


def spread(x, axes):
    n = lax.axis_size(axes)
    return lax.all_to_all(jnp.broadcast_to(x[None], (n,) + x.shape), axes, 0, 0, tiled=True)


def rows_times(a, b):
    return lax.dot_general(a, b, (((1,), (1,)), ((), ())), preferred_element_type=F32)


def times_rows(a, b):
    return lax.dot_general(a, b, (((0,), (0,)), ((), ())), preferred_element_type=F32)


def project_kernel(spot, fields, vectors, left, right, far, squares):
    value = times_rows(vectors[0], fields[0])
    squares[0] = jnp.sum(value * value, axis=1, keepdims=True)
    value = value.astype(BF16)
    half = value.shape[1] // 2
    left[...] = value[:, :half]
    right[...] = value[:, half:]
    far[...] = jnp.where(spot[1] // 2 == 0, value[:, half:], value[:, :half])


def project(spot, fields, vectors):
    runs, months, cells = fields.shape
    modes = vectors.shape[2]
    half = pl.BlockSpec((modes, cells // 2), lambda r, spot: (r, 0))
    out = jax.ShapeDtypeStruct((runs * modes, cells // 2), BF16)
    return pl.pallas_call(
        project_kernel,
        grid_spec=pltpu.PrefetchScalarGridSpec(
            num_scalar_prefetch=1,
            grid=(runs,),
            in_specs=[
                pl.BlockSpec((1, months, cells), lambda r, spot: (r, 0, 0)),
                pl.BlockSpec((1, months, modes), lambda r, spot: (r, 0, 0)),
            ],
            out_specs=[half] * 3 + [pl.BlockSpec((1, modes, 1), lambda r, spot: (r, 0, 0))],
        ),
        out_shape=[out] * 3 + [jax.ShapeDtypeStruct((runs, modes, 1), F32)],
        cost_estimate=pl.CostEstimate(
            flops=2 * runs * months * modes * cells,
            bytes_accessed=fields.size * 4,
            transcendentals=0,
        ),
        compiler_params=PARAMS,
    )(spot, fields, vectors)


def gram_kernel(fields, gram):
    months = fields.shape[1]
    gram[0] = jnp.zeros_like(gram[0])
    gram[0, :months, :months] = rows_times(fields[0], fields[0])


def gram_of(fields):
    runs, months, cells = fields.shape
    return pl.pallas_call(
        gram_kernel,
        grid=(runs,),
        in_specs=[pl.BlockSpec((1, months, cells), lambda r: (r, 0, 0))],
        out_specs=pl.BlockSpec((1, 128, 128), lambda r: (r, 0, 0)),
        out_shape=jax.ShapeDtypeStruct((runs, 128, 128), F32),
        cost_estimate=pl.CostEstimate(
            flops=2 * runs * months * months * cells,
            bytes_accessed=fields.size * 2,
            transcendentals=0,
        ),
        compiler_params=PARAMS,
    )(fields)


def pcs_kernel(first, second, mode, out):
    months, common = first.shape[1], mode.shape[0]
    wide = mode[...].astype(F32)
    norms = jnp.sum(wide * wide, axis=1, keepdims=True)
    out[0] = jnp.zeros_like(out[0])
    out[0, :common, :months] = rows_times(mode[...], first[0])
    out[0, common:, :months] = rows_times(mode[...], second[0])
    out[0, :common, months : months + 1] = norms
    out[0, common:, months : months + 1] = norms


def pcs_of(fields, mode):
    runs, months, cells = fields.shape
    return pl.pallas_call(
        pcs_kernel,
        grid=(runs // 2,),
        in_specs=[
            pl.BlockSpec((1, months, cells), lambda r: (r, 0, 0)),
            pl.BlockSpec((1, months, cells), lambda r: (r + 4, 0, 0)),
            pl.BlockSpec(mode.shape, lambda r: (0, 0)),
        ],
        out_specs=pl.BlockSpec((1, 128, 128), lambda r: (r, 0, 0)),
        out_shape=jax.ShapeDtypeStruct((runs // 2, 128, 128), F32),
        cost_estimate=pl.CostEstimate(
            flops=2 * fields.size * mode.shape[0],
            bytes_accessed=fields.size * 2,
            transcendentals=0,
        ),
        compiler_params=PARAMS,
    )(fields, fields, mode)


def put(spot, run, value, keep, send):
    value = value.astype(BF16)
    rows = value.shape[0]
    size = rows // 8

    def store(first, second):
        for x in range(4):
            for k in range(rows // 128):
                at = run * (rows // 128) + k
                columns = slice(k * 128, (k + 1) * 128)
                first[x, at] = value[x * size : (x + 1) * size, columns]
                second[x, at] = value[(x + 4) * size : (x + 5) * size, columns]

    @pl.when(spot[2] == 0)
    def _():
        store(keep, send)

    @pl.when(spot[2] != 0)
    def _():
        store(send, keep)


def put_product(spot, run, swapped, mine, theirs, keep, send):
    @pl.when(swapped == 0)
    def _():
        put(spot, run, rows_times(mine, theirs), keep, send)

    @pl.when(swapped != 0)
    def _():
        put(spot, run, rows_times(theirs, mine), keep, send)


def wrap(x):
    return lax.rem(x + 4, 4)


def chosen(flag, left, right):
    return jnp.where(flag == 0, left[...], right[...])


def near_kernel(spot, left, right, down, up, over, keep, send):
    b = spot[1]
    own = rows_times(left[...], left[...]) + rows_times(right[...], right[...])
    put(spot, b, own, keep, send)
    below, above, across = wrap(b + 1), wrap(b - 1), wrap(b + 2)
    middle = chosen(b // 2, left, right)
    for run, swapped, mine, theirs in (
        (below, (below < b).astype(jnp.int32), left[...], down),
        (above, (above < b).astype(jnp.int32), right[...], up),
        (across, b // 2, middle, over),
    ):
        put_product(spot, run, swapped, mine, theirs[...], keep, send)


def far_kernel(spot, left, right, z_left, z_right, down, up, over, keep, send):
    a, b = spot[0], spot[1]
    beside = chosen(a, z_left, z_right)
    middle = chosen(b // 2, left, right)
    for run, mine, theirs in (
        (b, chosen(a, left, right), beside),
        (wrap(b + 1), left[...], down[...]),
        (wrap(b - 1), right[...], up[...]),
        (wrap(b + 2), middle, over[...]),
    ):
        put_product(spot, run, a, mine, theirs, keep, send)


def blocks_of(kernel, spot, left, *others):
    rows, cells = left.shape
    out = jax.ShapeDtypeStruct((4, 4 * rows // 128, rows // 8, 128), BF16)
    whole = pl.BlockSpec(memory_space=pltpu.VMEM)
    return pl.pallas_call(
        kernel,
        in_specs=[pl.BlockSpec(memory_space=pltpu.SMEM)] + [whole] * (1 + len(others)),
        out_specs=[whole, whole],
        out_shape=[out, out],
        cost_estimate=pl.CostEstimate(
            flops=9 * rows * rows * cells, bytes_accessed=12 * left.size, transcendentals=0
        ),
        compiler_params=PARAMS,
    )(spot, left, *others)


def assemble_kernel(spot, own, other, row, col, out):
    j = pl.program_id(0)
    mine = spot[0] * 4 + spot[1]
    rows = out.shape[0]
    size, slabs = rows // 8, rows // 128
    here = pl.ds(pl.multiple_of(lax.rem(j, 2) * size * slabs, 16), size * slabs)
    parts = []
    for core in range(2):
        for x in range(4):
            held = jnp.where(spot[2] == core, own[x, 0, here], other[x, 0, here])
            parts.append(
                jnp.concatenate([held[k * size : (k + 1) * size] for k in range(slabs)], axis=1)
            )
    value = jnp.concatenate(parts, axis=0).astype(F32)

    @pl.when(j >= mine)
    def _():
        out[...] = value * row[...] * col[0]

    @pl.when(j < mine)
    def _():
        out[...] = value.T * row[...] * col[0]


def assemble(spot, own, other, row, col):
    rows = row.shape[0]
    held = pl.BlockSpec((4, 1) + own.shape[2:], lambda j, spot: (0, j // 2, 0, 0))
    return pl.pallas_call(
        assemble_kernel,
        grid_spec=pltpu.PrefetchScalarGridSpec(
            num_scalar_prefetch=1,
            grid=(8,),
            in_specs=[
                held,
                held,
                pl.BlockSpec((rows, 1), lambda j, spot: (0, 0)),
                pl.BlockSpec((1, 1, rows), lambda j, spot: (j, 0, 0)),
            ],
            out_specs=pl.BlockSpec((rows, rows), lambda j, spot: (0, j)),
        ),
        out_shape=jax.ShapeDtypeStruct((rows, 8 * rows), F32),
        compiler_params=PARAMS,
    )(spot, own, other, row, col)


def sum_of(parts):
    return jnp.sum(parts.astype(F32), axis=0)


def split(x):
    high = lax.reduce_precision(x, 8, 7)
    return jnp.concatenate([high.astype(BF16), (x - high).astype(BF16)], axis=0)


def scatter_x(parts):
    return sum_of(lax.all_to_all(parts, "x", 0, 0, tiled=True))


def together(work, *arrays):
    def nothing(*arrays):
        return jax.tree.map(lambda x: jnp.zeros(x.shape, x.dtype), jax.eval_shape(work, *arrays))

    return lax.cond(lax.axis_index("core") < 2, work, nothing, *arrays)


def per_device(fields, vectors, combos):
    runs, months, cells = fields.shape
    modes = vectors.shape[2]
    common = combos.shape[1]
    rows = runs * modes
    total = cells * lax.axis_size(CELLS)
    a, b, core = (lax.axis_index(name) for name in ("z_lo", "y", "core"))
    spot = jnp.stack([a, b, core]).astype(jnp.int32)
    barrier = lax.optimization_barrier

    left, right, far, squares = project(spot, fields, vectors)
    near = (send_to(left, 0, -1), send_to(right, 0, 1), send_to(far, 0, 2))
    z_left, z_right = send_to(left, 1, 0), send_to(right, 1, 0)
    weights = lax.dynamic_slice_in_dim(combos, lax.axis_index(RUNS) * rows, rows, 0)

    def scale_work(fields, squares):
        scale = jnp.sum(spread(squares.reshape(3, rows // 3), CELLS), axis=0)
        gram = gram_of(fields)
        gram_keep = jnp.where(core == 0, gram[:4], gram[4:])
        gram_send = jnp.where(core == 0, gram[4:], gram[:4])
        return scale.reshape(runs, modes) / total, gram_keep, gram_send

    def mode_work(fields, vectors, weights, scale, left, right, *near):
        keep, send = blocks_of(near_kernel, spot, left, right, *near)
        blocks = (keep.astype(F32) + swap_cores(send).astype(F32)).astype(BF16)
        blocks = scatter_x(blocks.reshape(4, rows * 3 // 2, 128)).astype(BF16)
        projected = jnp.einsum("rmk,rmc->rkc", vectors, fields, preferred_element_type=F32)
        basis = (projected * lax.rsqrt(scale)[:, :, None]).astype(BF16).reshape(rows, cells)
        part = times_rows(weights, basis).reshape(8, common // 8, cells)
        part = jnp.concatenate([part, jnp.broadcast_to(scale[None], (8, runs, modes))], axis=2)
        part, blocks = barrier((part, blocks))
        part = lax.all_to_all(part, RUNS, 0, 0, tiled=True)
        return basis, part, blocks

    scale, gram_keep, gram_send = together(scale_work, fields, squares)
    scale, z_left, z_right, *near = barrier((scale, z_left, z_right, *near))
    z_over = jnp.where(b // 2 == 0, z_right, z_left)
    far = (send_to(z_left, 0, -1), send_to(z_right, 0, 1), send_to(z_over, 0, 2))
    basis, part, near = together(
        mode_work, fields, vectors, weights, scale, left, right, *near
    )
    part, near, *far = barrier((part, near, *far))

    scales = part[:, :, cells:].reshape(8, rows)
    mode = spread(jnp.sum(part[:, :, :cells], axis=0).astype(BF16), RUNS)
    keep, send = blocks_of(far_kernel, spot, left, right, z_left, z_right, *far)
    blocks = (keep.astype(F32) + swap_cores(send).astype(F32)).astype(BF16)
    gram = (gram_keep + swap_cores(gram_send)).astype(BF16)
    mode = mode.reshape(common, cells)
    mode_wide = mode.astype(F32)
    pcs = pcs_of(fields, mode)
    pcs_keep = jnp.where(core == 0, pcs[:2], pcs[2:])
    pcs_send = jnp.where(core == 0, pcs[2:], pcs[:2])
    pcs = split(pcs_keep + swap_cores(pcs_send))
    extra = jnp.concatenate([gram, pcs], axis=0)
    extra = extra.reshape(8, 4, 32, 128).transpose(1, 0, 2, 3).reshape(4, 256, 128)

    half = rows * 3 // 2
    far = scatter_x(jnp.concatenate([blocks.reshape(4, half, 128), extra], axis=1))
    extra, far = far[half:], far[:half].astype(BF16)
    blocks = jnp.where(a == 0, jnp.concatenate([near, far]), jnp.concatenate([far, near]))
    blocks = blocks.reshape(8, half // 4, 128)
    others = lax.all_to_all(blocks, RUNS, 0, 0, tiled=True)
    same = lax.broadcasted_iota(jnp.int32, (8, 1, 1), 0) == a * 4 + b
    others = jnp.where(same, 0.0, others.astype(F32))
    blocks = (blocks.astype(F32) + others).astype(BF16).reshape(4, half // 2, 128)
    pcs = split(extra[128:192] + extra[192:]).reshape(2, 4, 16, 128)
    pieces = [blocks, extra[:128].astype(BF16).reshape(4, 32, 128), pcs[0], pcs[1]]
    pieces = jnp.concatenate(pieces, axis=1)
    pieces = sum_of(lax.all_to_all(pieces, "z_hi", 0, 0, tiled=True))
    pcs = split(pieces[-32:-16] + pieces[-16:])
    pieces = jnp.concatenate([pieces[:-32].astype(BF16), pcs], axis=0)
    own = spread(spread(pieces, "z_hi"), "x")
    other = swap_cores(own)
    row = lax.rsqrt(scale).reshape(rows, 1) / total
    col = lax.rsqrt(scales).reshape(8, 1, rows)
    merged = assemble(spot, own, other, row, col)

    def whole(pieces):
        extra = pieces[:, :, -64:].astype(F32)
        gram = extra[:, :, :32].transpose(1, 0, 2, 3).reshape(4, 128, 128)
        pcs = extra[:, :, 32:48] + extra[:, :, 48:]
        pcs = pcs.reshape(4, 2, 2, 16, 128).transpose(1, 0, 2, 3, 4).reshape(2, 128, 128)
        return gram, pcs

    both = [whole(own), whole(other)]
    gram, pcs = (
        jnp.where(
            core == 0,
            jnp.concatenate([both[0][n], both[1][n]]),
            jnp.concatenate([both[1][n], both[0][n]]),
        )
        for n in range(2)
    )
    gram = gram[:, :months, :months] / total
    pcs = pcs.reshape(runs // 2, 2, common, 128)
    inverse = lax.rsqrt(pcs[0, 0, :, months : months + 1] / total)
    pcs = (pcs[..., :months] * (inverse / total)).transpose(1, 0, 2, 3)
    pcs = pcs.reshape(runs, common, months).swapaxes(1, 2)
    eofs = (mode_wide * inverse).astype(BF16)
    return (gram, basis, merged, eofs, pcs)


def solution(mesh):
    fine = Mesh(mesh.devices.reshape(2, 4, 4, 4, 2), RUNS + CELLS)
    return jax.shard_map(
        per_device,
        mesh=fine,
        in_specs=(P(RUNS, None, CELLS), P(RUNS, None, None), P()),
        out_specs=(
            P(RUNS, None, None),
            P(RUNS, CELLS),
            P(RUNS, None),
            P(None, CELLS),
            P(RUNS, None, None),
        ),
        check_vma=False,
    )
```

```python
import jax
import jax.numpy as jnp
from jax import lax
from jax.experimental import pallas as pl
from jax.experimental.pallas import tpu as pltpu
from jax.sharding import Mesh
from jax.sharding import PartitionSpec as P

RUNS = ("z_lo", "y")
CELLS = ("x", "z_hi", "core")
F32 = jnp.float32
BF16 = jnp.bfloat16
PARAMS = pltpu.CompilerParams(vmem_limit_bytes=40 << 20)


def send_to(x, da, db):
    pairs = [
        (a * 4 + b, (a + da) % 2 * 4 + (b + db) % 4) for a in range(2) for b in range(4)
    ]
    return lax.ppermute(x, RUNS, pairs)


def swap_cores(x):
    return lax.ppermute(x, "core", [(0, 1), (1, 0)])


def spread(x, axes):
    n = lax.axis_size(axes)
    return lax.all_to_all(jnp.broadcast_to(x[None], (n,) + x.shape), axes, 0, 0, tiled=True)


def rows_times(a, b):
    return lax.dot_general(a, b, (((1,), (1,)), ((), ())), preferred_element_type=F32)


def times_rows(a, b):
    return lax.dot_general(a, b, (((0,), (0,)), ((), ())), preferred_element_type=F32)


def project_kernel(spot, fields, vectors, left, right, far, squares):
    value = times_rows(vectors[0], fields[0])
    squares[0] = jnp.sum(value * value, axis=1, keepdims=True)
    value = value.astype(BF16)
    half = value.shape[1] // 2
    left[...] = value[:, :half]
    right[...] = value[:, half:]
    far[...] = jnp.where(spot[1] // 2 == 0, value[:, half:], value[:, :half])


def project(spot, fields, vectors):
    runs, months, cells = fields.shape
    modes = vectors.shape[2]
    half = pl.BlockSpec((modes, cells // 2), lambda r, spot: (r, 0))
    out = jax.ShapeDtypeStruct((runs * modes, cells // 2), BF16)
    return pl.pallas_call(
        project_kernel,
        grid_spec=pltpu.PrefetchScalarGridSpec(
            num_scalar_prefetch=1,
            grid=(runs,),
            in_specs=[
                pl.BlockSpec((1, months, cells), lambda r, spot: (r, 0, 0)),
                pl.BlockSpec((1, months, modes), lambda r, spot: (r, 0, 0)),
            ],
            out_specs=[half] * 3 + [pl.BlockSpec((1, modes, 1), lambda r, spot: (r, 0, 0))],
        ),
        out_shape=[out] * 3 + [jax.ShapeDtypeStruct((runs, modes, 1), F32)],
        cost_estimate=pl.CostEstimate(
            flops=2 * runs * months * modes * cells,
            bytes_accessed=fields.size * 4,
            transcendentals=0,
        ),
        compiler_params=PARAMS,
    )(spot, fields, vectors)


def gram_kernel(fields, gram):
    months = fields.shape[1]
    gram[0] = jnp.zeros_like(gram[0])
    gram[0, :months, :months] = rows_times(fields[0], fields[0])


def gram_of(fields):
    runs, months, cells = fields.shape
    return pl.pallas_call(
        gram_kernel,
        grid=(runs,),
        in_specs=[pl.BlockSpec((1, months, cells), lambda r: (r, 0, 0))],
        out_specs=pl.BlockSpec((1, 128, 128), lambda r: (r, 0, 0)),
        out_shape=jax.ShapeDtypeStruct((runs, 128, 128), F32),
        cost_estimate=pl.CostEstimate(
            flops=2 * runs * months * months * cells,
            bytes_accessed=fields.size * 2,
            transcendentals=0,
        ),
        compiler_params=PARAMS,
    )(fields)


def pcs_kernel(first, second, mode, out):
    months, common = first.shape[1], mode.shape[0]
    wide = mode[...].astype(F32)
    norms = jnp.sum(wide * wide, axis=1, keepdims=True)
    out[0] = jnp.zeros_like(out[0])
    out[0, :common, :months] = rows_times(mode[...], first[0])
    out[0, common:, :months] = rows_times(mode[...], second[0])
    out[0, :common, months : months + 1] = norms
    out[0, common:, months : months + 1] = norms


def pcs_of(fields, mode):
    runs, months, cells = fields.shape
    return pl.pallas_call(
        pcs_kernel,
        grid=(runs // 2,),
        in_specs=[
            pl.BlockSpec((1, months, cells), lambda r: (r, 0, 0)),
            pl.BlockSpec((1, months, cells), lambda r: (r + 4, 0, 0)),
            pl.BlockSpec(mode.shape, lambda r: (0, 0)),
        ],
        out_specs=pl.BlockSpec((1, 128, 128), lambda r: (r, 0, 0)),
        out_shape=jax.ShapeDtypeStruct((runs // 2, 128, 128), F32),
        cost_estimate=pl.CostEstimate(
            flops=2 * fields.size * mode.shape[0],
            bytes_accessed=fields.size * 2,
            transcendentals=0,
        ),
        compiler_params=PARAMS,
    )(fields, fields, mode)


def put(spot, run, value, keep, send):
    value = value.astype(BF16)
    rows = value.shape[0]
    size = rows // 8

    def store(first, second):
        for x in range(4):
            for k in range(rows // 128):
                at = run * (rows // 128) + k
                columns = slice(k * 128, (k + 1) * 128)
                first[x, at] = value[x * size : (x + 1) * size, columns]
                second[x, at] = value[(x + 4) * size : (x + 5) * size, columns]

    @pl.when(spot[2] == 0)
    def _():
        store(keep, send)

    @pl.when(spot[2] != 0)
    def _():
        store(send, keep)


def put_product(spot, run, swapped, mine, theirs, keep, send):
    @pl.when(swapped == 0)
    def _():
        put(spot, run, rows_times(mine, theirs), keep, send)

    @pl.when(swapped != 0)
    def _():
        put(spot, run, rows_times(theirs, mine), keep, send)


def wrap(x):
    return lax.rem(x + 4, 4)


def chosen(flag, left, right):
    return jnp.where(flag == 0, left[...], right[...])


def near_kernel(spot, left, right, down, up, over, keep, send):
    b = spot[1]
    own = rows_times(left[...], left[...]) + rows_times(right[...], right[...])
    put(spot, b, own, keep, send)
    below, above, across = wrap(b + 1), wrap(b - 1), wrap(b + 2)
    middle = chosen(b // 2, left, right)
    for run, swapped, mine, theirs in (
        (below, (below < b).astype(jnp.int32), left[...], down),
        (above, (above < b).astype(jnp.int32), right[...], up),
        (across, b // 2, middle, over),
    ):
        put_product(spot, run, swapped, mine, theirs[...], keep, send)


def far_kernel(spot, left, right, z_left, z_right, down, up, over, keep, send):
    a, b = spot[0], spot[1]
    beside = chosen(a, z_left, z_right)
    middle = chosen(b // 2, left, right)
    for run, mine, theirs in (
        (b, chosen(a, left, right), beside),
        (wrap(b + 1), left[...], down[...]),
        (wrap(b - 1), right[...], up[...]),
        (wrap(b + 2), middle, over[...]),
    ):
        put_product(spot, run, a, mine, theirs, keep, send)


def blocks_of(kernel, spot, left, *others):
    rows, cells = left.shape
    out = jax.ShapeDtypeStruct((4, 4 * rows // 128, rows // 8, 128), BF16)
    whole = pl.BlockSpec(memory_space=pltpu.VMEM)
    return pl.pallas_call(
        kernel,
        in_specs=[pl.BlockSpec(memory_space=pltpu.SMEM)] + [whole] * (1 + len(others)),
        out_specs=[whole, whole],
        out_shape=[out, out],
        cost_estimate=pl.CostEstimate(
            flops=9 * rows * rows * cells, bytes_accessed=12 * left.size, transcendentals=0
        ),
        compiler_params=PARAMS,
    )(spot, left, *others)


def assemble_kernel(spot, own, other, row, col, out):
    j = pl.program_id(0)
    mine = spot[0] * 4 + spot[1]
    rows = out.shape[0]
    size, slabs = rows // 8, rows // 128
    here = pl.ds(pl.multiple_of(lax.rem(j, 2) * size * slabs, 16), size * slabs)
    parts = []
    for core in range(2):
        for x in range(4):
            held = jnp.where(spot[2] == core, own[x, 0, here], other[x, 0, here])
            parts.append(
                jnp.concatenate([held[k * size : (k + 1) * size] for k in range(slabs)], axis=1)
            )
    value = jnp.concatenate(parts, axis=0).astype(F32)

    @pl.when(j >= mine)
    def _():
        out[...] = value * row[...] * col[0]

    @pl.when(j < mine)
    def _():
        out[...] = value.T * row[...] * col[0]


def assemble(spot, own, other, row, col):
    rows = row.shape[0]
    held = pl.BlockSpec((4, 1) + own.shape[2:], lambda j, spot: (0, j // 2, 0, 0))
    return pl.pallas_call(
        assemble_kernel,
        grid_spec=pltpu.PrefetchScalarGridSpec(
            num_scalar_prefetch=1,
            grid=(8,),
            in_specs=[
                held,
                held,
                pl.BlockSpec((rows, 1), lambda j, spot: (0, 0)),
                pl.BlockSpec((1, 1, rows), lambda j, spot: (j, 0, 0)),
            ],
            out_specs=pl.BlockSpec((rows, rows), lambda j, spot: (0, j)),
        ),
        out_shape=jax.ShapeDtypeStruct((rows, 8 * rows), F32),
        compiler_params=PARAMS,
    )(spot, own, other, row, col)


def sum_of(parts):
    return jnp.sum(parts.astype(F32), axis=0)


def split(x):
    high = lax.reduce_precision(x, 8, 7)
    return jnp.concatenate([high.astype(BF16), (x - high).astype(BF16)], axis=0)


def scatter_x(parts):
    return sum_of(lax.all_to_all(parts, "x", 0, 0, tiled=True))


def together(work, *arrays):
    def nothing(*arrays):
        return jax.tree.map(lambda x: jnp.zeros(x.shape, x.dtype), jax.eval_shape(work, *arrays))

    return lax.cond(lax.axis_index("core") < 2, work, nothing, *arrays)


def per_device(fields, vectors, combos):
    runs, months, cells = fields.shape
    modes = vectors.shape[2]
    common = combos.shape[1]
    rows = runs * modes
    total = cells * lax.axis_size(CELLS)
    a, b, core = (lax.axis_index(name) for name in ("z_lo", "y", "core"))
    spot = jnp.stack([a, b, core]).astype(jnp.int32)
    barrier = lax.optimization_barrier

    left, right, far, squares = project(spot, fields, vectors)
    near = (send_to(left, 0, -1), send_to(right, 0, 1), send_to(far, 0, 2))
    z_left, z_right = send_to(left, 1, 0), send_to(right, 1, 0)
    weights = lax.dynamic_slice_in_dim(combos, lax.axis_index(RUNS) * rows, rows, 0)

    def scale_work(fields, squares):
        scale = jnp.sum(spread(squares.reshape(3, rows // 3), CELLS), axis=0)
        gram = gram_of(fields)
        gram_keep = jnp.where(core == 0, gram[:4], gram[4:])
        gram_send = jnp.where(core == 0, gram[4:], gram[:4])
        return scale.reshape(runs, modes) / total, gram_keep, gram_send

    def mode_work(fields, vectors, weights, scale, left, right, *near):
        keep, send = blocks_of(near_kernel, spot, left, right, *near)
        blocks = (keep.astype(F32) + swap_cores(send).astype(F32)).astype(BF16)
        fields, blocks = barrier((fields, blocks))
        blocks = scatter_x(blocks.reshape(4, rows * 3 // 2, 128)).astype(BF16)
        projected = jnp.einsum("rmk,rmc->rkc", vectors, fields, preferred_element_type=F32)
        basis = (projected * lax.rsqrt(scale)[:, :, None]).astype(BF16).reshape(rows, cells)
        part = times_rows(weights, basis).reshape(8, common // 8, cells)
        part = jnp.concatenate([part, jnp.broadcast_to(scale[None], (8, runs, modes))], axis=2)
        part, blocks = barrier((part, blocks))
        part = lax.all_to_all(part, RUNS, 0, 0, tiled=True)
        return basis, part, blocks

    scale, gram_keep, gram_send = together(scale_work, fields, squares)
    scale, z_left, z_right, *near = barrier((scale, z_left, z_right, *near))
    z_over = jnp.where(b // 2 == 0, z_right, z_left)
    far = (send_to(z_left, 0, -1), send_to(z_right, 0, 1), send_to(z_over, 0, 2))
    basis, part, near = together(
        mode_work, fields, vectors, weights, scale, left, right, *near
    )
    part, near, *far = barrier((part, near, *far))

    scales = part[:, :, cells:].reshape(8, rows)
    mode = spread(jnp.sum(part[:, :, :cells], axis=0).astype(BF16), RUNS)
    keep, send = blocks_of(far_kernel, spot, left, right, z_left, z_right, *far)
    blocks = (keep.astype(F32) + swap_cores(send).astype(F32)).astype(BF16)
    gram = (gram_keep + swap_cores(gram_send)).astype(BF16)
    mode = mode.reshape(common, cells)
    mode_wide = mode.astype(F32)
    pcs = pcs_of(fields, mode)
    pcs_keep = jnp.where(core == 0, pcs[:2], pcs[2:])
    pcs_send = jnp.where(core == 0, pcs[2:], pcs[:2])
    pcs = split(pcs_keep + swap_cores(pcs_send))
    extra = jnp.concatenate([gram, pcs], axis=0)
    extra = extra.reshape(8, 4, 32, 128).transpose(1, 0, 2, 3).reshape(4, 256, 128)

    half = rows * 3 // 2
    far = scatter_x(jnp.concatenate([blocks.reshape(4, half, 128), extra], axis=1))
    extra, far = far[half:], far[:half].astype(BF16)
    blocks = jnp.where(a == 0, jnp.concatenate([near, far]), jnp.concatenate([far, near]))
    blocks = blocks.reshape(8, half // 4, 128)
    others = lax.all_to_all(blocks, RUNS, 0, 0, tiled=True)
    same = lax.broadcasted_iota(jnp.int32, (8, 1, 1), 0) == a * 4 + b
    others = jnp.where(same, 0.0, others.astype(F32))
    blocks = (blocks.astype(F32) + others).astype(BF16).reshape(4, half // 2, 128)
    pcs = split(extra[128:192] + extra[192:]).reshape(2, 4, 16, 128)
    pieces = [blocks, extra[:128].astype(BF16).reshape(4, 32, 128), pcs[0], pcs[1]]
    pieces = jnp.concatenate(pieces, axis=1)
    pieces = sum_of(lax.all_to_all(pieces, "z_hi", 0, 0, tiled=True))
    pcs = split(pieces[-32:-16] + pieces[-16:])
    pieces = jnp.concatenate([pieces[:-32].astype(BF16), pcs], axis=0)
    own = spread(spread(pieces, "z_hi"), "x")
    other = swap_cores(own)
    row = lax.rsqrt(scale).reshape(rows, 1) / total
    col = lax.rsqrt(scales).reshape(8, 1, rows)
    merged = assemble(spot, own, other, row, col)

    def whole(pieces):
        extra = pieces[:, :, -64:].astype(F32)
        gram = extra[:, :, :32].transpose(1, 0, 2, 3).reshape(4, 128, 128)
        pcs = extra[:, :, 32:48] + extra[:, :, 48:]
        pcs = pcs.reshape(4, 2, 2, 16, 128).transpose(1, 0, 2, 3, 4).reshape(2, 128, 128)
        return gram, pcs

    both = [whole(own), whole(other)]
    gram, pcs = (
        jnp.where(
            core == 0,
            jnp.concatenate([both[0][n], both[1][n]]),
            jnp.concatenate([both[1][n], both[0][n]]),
        )
        for n in range(2)
    )
    gram = gram[:, :months, :months] / total
    pcs = pcs.reshape(runs // 2, 2, common, 128)
    inverse = lax.rsqrt(pcs[0, 0, :, months : months + 1] / total)
    pcs = (pcs[..., :months] * (inverse / total)).transpose(1, 0, 2, 3)
    pcs = pcs.reshape(runs, common, months).swapaxes(1, 2)
    eofs = (mode_wide * inverse).astype(BF16)
    return (gram, basis, merged, eofs, pcs)


def solution(mesh):
    fine = Mesh(mesh.devices.reshape(2, 4, 4, 4, 2), RUNS + CELLS)
    return jax.shard_map(
        per_device,
        mesh=fine,
        in_specs=(P(RUNS, None, CELLS), P(RUNS, None, None), P()),
        out_specs=(
            P(RUNS, None, None),
            P(RUNS, CELLS),
            P(RUNS, None),
            P(None, CELLS),
            P(RUNS, None, None),
        ),
        check_vma=False,
    )
```
